32 devices in a mesh: guid: 2 (over x), req: 4 (over y, core), seq: 4 (over z).
Axes of the slice: x: 2, y: 2, z: 4, core: 2. Of those that a mesh axis runs over, the one named last changes fastest.
Arguments:
- img_hidden: bfloat16 [2, 24, 1024, 1536], P('guid', 'req', 'seq'), may hold values from -6 to 6
- txt_hidden: bfloat16 [2, 24, 192, 1536], P('guid', 'req', 'seq'), may hold values from -6 to 6
- img_mod: float32 [2, 24, 5, 1536], P('guid', 'req')
- txt_mod: float32 [2, 24, 2, 1536], P('guid', 'req'), may hold values from -3 to 3
- w_img_qkv: bfloat16 [1536, 3072], P(('guid', 'req', 'seq')), may hold values from -0.15625 to 0.15625
- w_txt_qkv: bfloat16 [1536, 3072], P(('guid', 'req', 'seq')), may hold values from -0.15625 to 0.15625
- w_out: bfloat16 [1024, 1536], P(('guid', 'req', 'seq')), may hold values from -0.1875 to 0.1875
- w_head: bfloat16 [1536, 64], P(('guid', 'req', 'seq')), may hold values from -0.15625 to 0.15625
- text_lengths: int32 [2, 24], P('guid', 'req'), may hold values from 1 to 154, as said below
- latent: float32 [24, 1024, 64], P('req', 'seq', 'guid'), may hold values from -6 to 6
- step: int32 [1], replicated, may hold values from 0 to 27
Outputs:
- advanced: float32 [24, 1024, 64], P('req', 'seq', 'guid')
- guided: float32 [24, 1024, 64], P('req', 'seq', 'guid')
The draws below stay inside these ranges and needn't reach their ends.
Inputs may be any that keep to these rules, and one draw needn't show every extreme that they name: `text_lengths`: in each half one prompt has 154 text tokens and another has 1.
All inputs are finite; a program needn't handle non-finite values.
Results may differ from the reference program's by a relative error of at most 0.012.
The reference program's roundings to bfloat16 on the way count: a program that leaves them out, or rounds other values in their place, can miss the bound.
Values may be sent and summed in bfloat16 or wider, within the bound.
A program may use at most 256 MiB of HBM per device.

```python
import jax
import jax.numpy as jnp
from jax import lax

D = 1536
HEADS = 16
HD = 64
IMG = 1024
TXT = 192
TXT_MAX = 154
PATCH = 64
STEPS = 28
PROMPTS = 24
AW = 1024


def draw_img_mod(key, part):
    sample = 0.5 * jax.random.normal(key, (2, PROMPTS, 5, D), jnp.float32)
    return sample


def draw_text_lengths(key, part):
    sample = jax.random.randint(key, (2, PROMPTS), 1, TXT_MAX + 1)
    chosen = jax.random.randint(jax.random.fold_in(key, 3), (2, 1), 0, PROMPTS)
    places = jnp.arange(PROMPTS)[None, :]
    sample = jnp.where(places == chosen, TXT_MAX, sample)
    sample = jnp.where(places == (chosen + 1) % PROMPTS, 1, sample)
    return sample.astype(jnp.int32)


def level_of(own_key, dims, cuts, least, high):
    factor_of = 1.0
    for axis_at, parts in cuts:
        heights = jax.random.uniform(jax.random.fold_in(jax.random.fold_in(own_key, 6), axis_at), (parts,), jnp.float32, least / len(cuts), high / len(cuts))
        factor_of = factor_of * jnp.repeat(jnp.exp(heights), dims[axis_at] // parts).reshape((-1,) + (1,) * (len(dims) - 1 - axis_at))
    return factor_of


def noise(own_key, shape, scale, limit, split=(), held_as=jnp.bfloat16):
    entries = scale * jax.random.normal(own_key, shape, jnp.float32)
    if split:
        entries = entries * level_of(own_key, shape, split, -0.22, 0.18)
    return jnp.clip(entries, -limit, limit).astype(held_as)


def setup_inputs(seed: int = 0) -> dict:
    keys = jax.random.split(jax.random.key(seed), 12)
    return {
        "img_hidden": noise(keys[0], (2, PROMPTS, IMG, D), 1.0, 6.0, ((0, 2), (1, 4), (2, 4))),
        "txt_hidden": noise(keys[1], (2, PROMPTS, TXT, D), 1.0, 6.0, ((0, 2), (1, 4), (2, 4))),
        "img_mod": draw_img_mod(jax.random.fold_in(keys[11], 71), 0),
        "txt_mod": noise(keys[3], (2, PROMPTS, 2, D), 0.5, 3.0, ((0, 2), (1, 4)), jnp.float32),
        "w_img_qkv": noise(keys[4], (D, 3 * AW), D ** -0.5, 0.15625, ((0, 32),)),
        "w_txt_qkv": noise(keys[5], (D, 3 * AW), D ** -0.5, 0.15625, ((0, 32),)),
        "w_out": noise(keys[6], (AW, D), AW ** -0.5, 0.1875, ((0, 32),)),
        "w_head": noise(keys[7], (D, PATCH), D ** -0.5, 0.15625, ((0, 32),)),
        "text_lengths": draw_text_lengths(jax.random.fold_in(keys[11], 71), 0),
        "latent": noise(keys[9], (PROMPTS, IMG, PATCH), 1.0, 6.0, ((0, 4), (1, 4), (2, 2)), jnp.float32),
        "step": jax.random.randint(keys[10], (1,), 0, STEPS).astype(jnp.int32),
    }


norm_epsilon = 1e-06
flow_shift = 3.0
guide_scale = 4.5

def modulate(values_in, shift_vec, scale_vec):
    values_in = values_in.astype(jnp.float32)
    average = lax.optimization_barrier(jnp.mean(values_in, axis=-1, keepdims=True))
    variance = lax.optimization_barrier(jnp.mean((values_in - average) ** 2, axis=-1, keepdims=True))
    normed = (values_in - average) * lax.rsqrt(variance + norm_epsilon)
    return (normed * (1.0 + scale_vec[..., None, :]) + shift_vec[..., None, :]).astype(jnp.bfloat16)

def sigma_level(step_value):
    remaining = 1.0 - step_value / STEPS
    return flow_shift * remaining / (1.0 + (flow_shift - 1.0) * remaining)

def reference(img_hidden, txt_hidden, img_mod, txt_mod, w_img_qkv, w_txt_qkv, w_out, w_head, text_lengths, latent, step):
    attn_width = w_out.shape[0]
    image_in = modulate(img_hidden, img_mod[:, :, 0], img_mod[:, :, 1])
    text_in = modulate(txt_hidden, txt_mod[:, :, 0], txt_mod[:, :, 1])

    def per_prompt(members):
        image_rows, text_rows, modulation, hidden, length = members
        qkv_image = lax.optimization_barrier(jnp.dot(image_rows, w_img_qkv, preferred_element_type=jnp.float32).astype(jnp.bfloat16))
        qkv_text = lax.optimization_barrier(jnp.dot(text_rows, w_txt_qkv, preferred_element_type=jnp.float32).astype(jnp.bfloat16))
        query_rows = qkv_image[:, :attn_width].astype(jnp.float32).reshape(IMG, HEADS, HD)
        key_rows = jnp.concatenate([qkv_image[:, attn_width:2 * attn_width], qkv_text[:, attn_width:2 * attn_width]], axis=0)
        value_rows = jnp.concatenate([qkv_image[:, 2 * attn_width:], qkv_text[:, 2 * attn_width:]], axis=0)
        key_rows = key_rows.astype(jnp.float32).reshape(IMG + TXT, HEADS, HD)
        value_rows = value_rows.astype(jnp.float32).reshape(IMG + TXT, HEADS, HD)
        allowed = jnp.concatenate([jnp.ones((IMG,), bool), jnp.arange(TXT, dtype=jnp.int32) < length])
        scores = jnp.einsum('qhd,khd->hqk', query_rows, key_rows) * 0.125
        scores = jnp.where(allowed[None, None, :], scores, -1e+30)
        highest = lax.optimization_barrier(jnp.max(scores, axis=-1, keepdims=True))
        weights = jnp.exp(scores - highest)
        totals = lax.optimization_barrier(jnp.sum(weights, axis=-1))
        rounded = lax.optimization_barrier(weights.astype(jnp.bfloat16)).astype(jnp.float32)
        mixture = jnp.einsum('hqk,khd->qhd', rounded, value_rows) / jnp.transpose(totals)[:, :, None]
        attended = mixture.reshape(IMG, attn_width).astype(jnp.bfloat16)
        projected = jnp.dot(attended, w_out, preferred_element_type=jnp.float32)
        residual = hidden.astype(jnp.float32) + modulation[2][None, :] * projected
        final_in = modulate(residual, modulation[3], modulation[4])
        return jnp.dot(final_in, w_head, preferred_element_type=jnp.float32)
    count_all = 2 * PROMPTS
    velocity = lax.map(per_prompt, (image_in.reshape(count_all, IMG, D), text_in.reshape(count_all, TXT, D), img_mod.reshape(count_all, 5, D), img_hidden.reshape(count_all, IMG, D), text_lengths.reshape(count_all)))
    velocity = velocity.reshape(2, PROMPTS, IMG, PATCH)
    guided = velocity[1] + guide_scale * (velocity[0] - velocity[1])
    step_value = step[0].astype(jnp.float32)
    advanced = latent + (sigma_level(step_value + 1.0) - sigma_level(step_value)) * guided
    return (advanced, guided)
```

```python
import functools

import jax
import jax.numpy as jnp
from jax import lax
from jax.experimental import pallas as pl
from jax.experimental.pallas import tpu as pltpu
from jax.sharding import PartitionSpec as P

HD = 64
STEPS = 28


norm_epsilon = 1e-06
flow_shift = 3.0
guide_scale = 4.5


def partner(value, axis, bit):
    mask = 2**bit
    pairs = [(source, source ^ mask) for source in range(lax.axis_size(axis))]
    return lax.ppermute(value, axis, pairs)


def modulate(values_in, shift_vec, scale_vec):
    values_in = values_in.astype(jnp.float32)
    average = jnp.mean(values_in, axis=-1, keepdims=True)
    variance = jnp.mean((values_in - average) ** 2, axis=-1, keepdims=True)
    normed = (values_in - average) * lax.rsqrt(variance + norm_epsilon)
    return (normed * (1.0 + scale_vec[..., None, :]) + shift_vec[..., None, :]).astype(jnp.bfloat16)


def sigma_level(step_value):
    remaining = 1.0 - step_value / STEPS
    return flow_shift * remaining / (1.0 + (flow_shift - 1.0) * remaining)


def local(
    img_hidden,
    txt_hidden,
    img_mod,
    txt_mod,
    w_img_qkv,
    w_txt_qkv,
    w_out,
    w_head,
    text_lengths,
    latent,
    step,
):
    prompts = img_hidden.shape[1]
    img_rows = img_hidden.shape[2]
    txt_rows = txt_hidden.shape[2]
    dev_rows = img_rows + txt_rows
    model_width = img_hidden.shape[3]
    image_in = modulate(img_hidden[0], img_mod[0, :, 0], img_mod[0, :, 1])
    text_in = modulate(txt_hidden[0], txt_mod[0, :, 0], txt_mod[0, :, 1])
    full_img, full_txt, full_head = (
        lax.all_gather(w_img_qkv, ("guid", "req", "seq"), axis=0, tiled=True),
        lax.all_gather(w_txt_qkv, ("guid", "req", "seq"), axis=0, tiled=True),
        lax.all_gather(w_head, ("guid", "req", "seq"), axis=0, tiled=True),
    )
    attn_width = full_img.shape[1] // 3
    head_count = attn_width // HD
    qkv_image = jnp.einsum(
        "prd,de->pre", image_in, full_img, preferred_element_type=jnp.float32
    ).astype(jnp.bfloat16)
    qkv_text = jnp.einsum(
        "prd,de->pre", text_in, full_txt, preferred_element_type=jnp.float32
    ).astype(jnp.bfloat16)
    query_rows = qkv_image[..., :attn_width]
    key_rows = jnp.concatenate(
        [qkv_image[..., attn_width : 2 * attn_width], qkv_text[..., attn_width : 2 * attn_width]],
        axis=1,
    )
    value_rows = jnp.concatenate(
        [qkv_image[..., 2 * attn_width :], qkv_text[..., 2 * attn_width :]], axis=1
    )
    lengths = text_lengths[0]
    query_heads = query_rows.reshape(prompts, img_rows, head_count, HD)
    running = jnp.full((prompts, head_count, img_rows), -1e30, jnp.float32)
    key_piece = lax.all_gather(key_rows, "seq", axis=1, tiled=True)
    value_piece = lax.all_gather(value_rows, "seq", axis=1, tiled=True)
    piece_rows = key_piece.shape[1]
    key_heads = key_piece.reshape(prompts, piece_rows, head_count, HD)
    value_heads = value_piece.reshape(prompts, piece_rows, head_count, HD)
    scores = (
        jnp.einsum("pqhd,pkhd->phqk", query_heads, key_heads, preferred_element_type=jnp.float32)
        * 0.125
    )
    position = jnp.arange(piece_rows, dtype=jnp.int32)
    owner_dev = position // dev_rows
    offset = position % dev_rows
    text_pos = owner_dev * txt_rows + offset - img_rows
    allowed = (offset < img_rows)[None, :] | (text_pos[None, :] < lengths[:, None])
    scores = jnp.where(allowed[:, None, None, :], scores, -1e30)
    newest = jnp.maximum(running, jnp.max(scores, axis=-1))
    weights = jnp.exp(scores - newest[..., None])
    totals = jnp.sum(weights, axis=-1)
    accumulated = jnp.einsum(
        "phqk,pkhd->phqd",
        weights.astype(jnp.bfloat16),
        value_heads,
        preferred_element_type=jnp.float32,
    )
    running, totals, accumulated = (newest, totals, accumulated)
    mixture = accumulated / totals[..., None]
    attended = (
        jnp.transpose(mixture, (0, 2, 1, 3))
        .reshape(prompts, img_rows, attn_width)
        .astype(jnp.bfloat16)
    )
    flattened = attended.reshape(prompts * img_rows, attn_width)
    full_out = lax.all_gather(w_out, ("guid", "req", "seq"), axis=0, tiled=True)
    projected = jnp.dot(flattened, full_out, preferred_element_type=jnp.float32)
    residual = img_hidden[0].astype(jnp.float32) + img_mod[0, :, 2][:, None, :] * projected.reshape(
        prompts, img_rows, model_width
    )
    final_in = modulate(residual, img_mod[0, :, 3], img_mod[0, :, 4])
    guid_index = lax.axis_index("guid")
    half_width = latent.shape[2]
    own_start = guid_index * half_width
    other_start = (1 - guid_index) * half_width
    whole_velocity = jnp.einsum(
        "prd,dc->prc", final_in, full_head, preferred_element_type=jnp.float32
    )
    own_velocity = lax.dynamic_slice_in_dim(whole_velocity, own_start, half_width, 2)
    partner_part = lax.dynamic_slice_in_dim(whole_velocity, other_start, half_width, 2)
    other_velocity = partner(partner_part.astype(jnp.bfloat16), "guid", 0).astype(
        partner_part.dtype
    )
    cond_velocity = jnp.where(guid_index == 0, own_velocity, other_velocity)
    free_velocity = jnp.where(guid_index == 0, other_velocity, own_velocity)
    guided = free_velocity + guide_scale * (cond_velocity - free_velocity)
    step_value = step[0].astype(jnp.float32)
    advanced = latent + (sigma_level(step_value + 1.0) - sigma_level(step_value)) * guided
    return (advanced, guided)


ALL_AXES = ("guid", "req", "seq")
LOG2E = 1.4426950408889634


def attend_kernel(images, texts, *refs):
    q_ref, o_ref = refs[0], refs[-1]
    pieces = []
    at = 1
    for _ in range(images):
        pieces.append((refs[at], refs[at + 1], None))
        at += 2
    for _ in range(texts):
        pieces.append((refs[at], refs[at + 1], refs[at + 2]))
        at += 3
    q = q_ref[...] * jnp.asarray(0.125, jnp.bfloat16)
    lane = lax.broadcasted_iota(jnp.int32, q.shape, 1)
    halves = []
    for head in range(2):
        mine = (lane < HD) if head == 0 else (lane >= HD)
        q_head = jnp.where(mine, q, jnp.zeros_like(q))
        scores = []
        for k_ref, _, bias_ref in pieces:
            s = lax.dot_general(
                q_head, k_ref[...], (((1,), (1,)), ((), ())), preferred_element_type=jnp.float32
            )
            if bias_ref is not None:
                s = s + bias_ref[0:1, :]
            scores.append(s)
        top = functools.reduce(jnp.maximum, [jnp.max(s, axis=1, keepdims=True) for s in scores])
        top = top * LOG2E
        total = None
        mixed = None
        for s, (_, v_ref, _) in zip(scores, pieces):
            p = jnp.exp2(s * LOG2E - top)
            part = jnp.sum(p, axis=1, keepdims=True)
            total = part if total is None else total + part
            part = jnp.dot(p.astype(jnp.bfloat16), v_ref[...], preferred_element_type=jnp.float32)
            mixed = part if mixed is None else mixed + part
        halves.append(mixed / total)
    o_ref[...] = jnp.where(lane < HD, halves[0], halves[1]).astype(jnp.bfloat16)


def attend(query, width, images, texts):
    rows = query.shape[0]
    block = min(256, rows)
    pairs = width // 128
    args = [query]
    specs = [pl.BlockSpec((block, 128), lambda h, i: (i, h))]

    def column(array, start):
        args.append(array)
        specs.append(pl.BlockSpec((array.shape[0], 128), lambda h, i: (0, start // 128 + h)))

    keys = 0
    for array, key_at, value_at in images:
        column(array, key_at)
        column(array, value_at)
        keys += array.shape[0]
    for array, key_at, value_at, bias in texts:
        column(array, key_at)
        column(array, value_at)
        args.append(bias)
        specs.append(pl.BlockSpec(bias.shape, lambda h, i: (0, 0)))
        keys += array.shape[0]
    return pl.pallas_call(
        functools.partial(attend_kernel, len(images), len(texts)),
        grid=(pairs, rows // block),
        in_specs=specs,
        out_specs=pl.BlockSpec((block, 128), lambda h, i: (i, h)),
        out_shape=jax.ShapeDtypeStruct((rows, width), jnp.bfloat16),
        compiler_params=pltpu.CompilerParams(vmem_limit_bytes=28 * 2**20),
        cost_estimate=pl.CostEstimate(
            flops=16 * rows * keys * width,
            bytes_accessed=4 * (rows + keys) * width,
            transcendentals=rows * keys * width // HD,
        ),
    )(*args)


def text_bias(position, length):
    bias = jnp.where(position < length, 0.0, -1e30).astype(jnp.float32)
    return jnp.broadcast_to(bias[None, :], (8, bias.shape[0]))


def moved(
    img_hidden,
    txt_hidden,
    img_mod,
    txt_mod,
    w_img_qkv,
    w_txt_qkv,
    w_out,
    w_head,
    text_lengths,
    latent,
    step,
):
    ranks = lax.axis_size("seq")
    seq = lax.axis_index("seq")
    core = lax.axis_index("req") % 2
    guid = lax.axis_index("guid")
    attn_width = w_out.shape[0] * lax.axis_size(ALL_AXES)
    model_width = img_hidden.shape[3]
    img_rows, txt_rows = img_hidden.shape[2], txt_hidden.shape[2]
    img_half, txt_half = img_rows // 2, txt_rows // 2

    def swap(value):
        count = lax.axis_size("req")
        return lax.ppermute(value, "req", [(r, r ^ 1) for r in range(count)])

    def hop(value, k):
        return lax.ppermute(value, "seq", [(r, r ^ k) for r in range(ranks)])

    def pick(value, index):
        return lax.dynamic_index_in_dim(value, index, 0, keepdims=False)

    def spread(value):
        return [pick(value, seq)] + [hop(pick(value, seq ^ k), k) for k in range(1, ranks)]

    def by_core(mine, other, axis):
        return jnp.where(
            core == 0,
            jnp.concatenate([mine, other], axis),
            jnp.concatenate([other, mine], axis),
        )

    def halved(value, rows):
        kept = lax.dynamic_slice_in_dim(value, core * rows, rows, 1)
        sent = lax.dynamic_slice_in_dim(value, (1 - core) * rows, rows, 1)
        return by_core(kept, swap(sent), 0)

    full_img = lax.all_gather(w_img_qkv, ALL_AXES, axis=0, tiled=True)
    full_txt = lax.all_gather(w_txt_qkv[:, attn_width:], ALL_AXES, axis=0, tiled=True)
    head_lines = w_head.size // model_width
    tail = jnp.concatenate([w_out, w_head.reshape(head_lines, model_width)], 0)
    full_tail = lax.all_gather(tail, ALL_AXES, axis=0, tiled=False)
    full_out = full_tail[:, : w_out.shape[0]].reshape(attn_width, model_width)
    full_head = full_tail[:, w_out.shape[0] :].reshape(model_width, w_head.shape[1])

    img_own = jnp.concatenate(spread(img_hidden[0, :ranks]), 0)
    txt_own = jnp.concatenate(spread(txt_hidden[0, :ranks]), 0)
    img_pair = jnp.concatenate(spread(halved(img_hidden[0, ranks:], img_half)), 0)
    txt_pair = jnp.concatenate(spread(halved(txt_hidden[0, ranks:], txt_half)), 0)
    mod_own, tmod_own, len_own = pick(img_mod[0], seq), pick(txt_mod[0], seq), pick(text_lengths[0], seq)
    mod_pair = pick(by_core(img_mod[0, ranks:], swap(img_mod[0, ranks:]), 0), seq)
    tmod_pair = pick(by_core(txt_mod[0, ranks:], swap(txt_mod[0, ranks:]), 0), seq)
    len_pair = pick(by_core(text_lengths[0, ranks:], swap(text_lengths[0, ranks:]), 0), seq)

    def dot(left, right):
        return jnp.dot(left, right, preferred_element_type=jnp.float32)

    def places(start, count):
        slots = jnp.arange(ranks, dtype=jnp.int32) ^ seq
        return (slots[:, None] * txt_rows + start + jnp.arange(count, dtype=jnp.int32)[None]).reshape(-1)

    qkv_own = dot(modulate(img_own, mod_own[0], mod_own[1]), full_img).astype(jnp.bfloat16)
    kvt_own = dot(modulate(txt_own, tmod_own[0], tmod_own[1]), full_txt).astype(jnp.bfloat16)
    qkv_pair = dot(modulate(img_pair, mod_pair[0], mod_pair[1]), full_img).astype(jnp.bfloat16)
    kvt_pair = dot(modulate(txt_pair, tmod_pair[0], tmod_pair[1]), full_txt).astype(jnp.bfloat16)
    kv_other = swap(qkv_pair[:, attn_width:])
    kvt_other = swap(kvt_pair)

    attended_own = attend(
        qkv_own,
        attn_width,
        [(qkv_own, attn_width, 2 * attn_width)],
        [(kvt_own, 0, attn_width, text_bias(places(0, txt_rows), len_own))],
    )
    attended_pair = attend(
        qkv_pair,
        attn_width,
        [(qkv_pair, attn_width, 2 * attn_width), (kv_other, 0, attn_width)],
        [
            (kvt_pair, 0, attn_width, text_bias(places(core * txt_half, txt_half), len_pair)),
            (kvt_other, 0, attn_width, text_bias(places((1 - core) * txt_half, txt_half), len_pair)),
        ],
    )

    def finish(attended, hidden, mod):
        residual = hidden.astype(jnp.float32) + mod[2] * dot(attended, full_out)
        return dot(modulate(residual, mod[3], mod[4]), full_head)

    velocity = jnp.concatenate(
        [
            finish(attended_own, img_own, mod_own).reshape(ranks, img_rows, -1),
            finish(attended_pair, img_pair, mod_pair).reshape(ranks, img_half, -1),
        ],
        1,
    )
    part = latent.shape[2]
    own = lax.dynamic_slice_in_dim(velocity, guid * part, part, 2)
    sent = lax.dynamic_slice_in_dim(velocity, (1 - guid) * part, part, 2).astype(jnp.bfloat16)
    other = partner(sent, "guid", 0).astype(jnp.float32)
    cond = jnp.where(guid == 0, own, other)
    free = jnp.where(guid == 0, other, own)
    guided = free + guide_scale * (cond - free)
    back = jnp.stack([guided[0]] + [hop(guided[k], k) for k in range(1, ranks)])
    back = jnp.stack([pick(back, seq ^ p) for p in range(ranks)])
    shared = back[:, img_rows:]
    kept = lax.dynamic_slice_in_dim(shared, core * (ranks // 2), ranks // 2, 0)
    given = lax.dynamic_slice_in_dim(shared, (1 - core) * (ranks // 2), ranks // 2, 0)
    guided = jnp.concatenate([back[:, :img_rows], by_core(kept, swap(given), 1)], 0)
    step_value = step[0].astype(jnp.float32)
    advanced = latent + (sigma_level(step_value + 1.0) - sigma_level(step_value)) * guided
    return (advanced, guided)


def block(img_hidden, *others):
    ranks = lax.axis_size("seq")
    if ranks & (ranks - 1) == 0 and 2 * img_hidden.shape[1] == 3 * ranks and lax.axis_size("req") % 2 == 0:
        return moved(img_hidden, *others)
    return local(img_hidden, *others)


def solution(mesh):
    placed = (
        P("guid", "req", "seq", None),
        P("guid", "req", "seq", None),
        P("guid", "req", None, None),
        P("guid", "req", None, None),
        P(("guid", "req", "seq"), None),
        P(("guid", "req", "seq"), None),
        P(("guid", "req", "seq"), None),
        P(("guid", "req", "seq"), None),
        P("guid", "req"),
        P("req", "seq", "guid"),
        P(),
    )
    return jax.shard_map(
        block,
        mesh=mesh,
        in_specs=placed,
        out_specs=(P("req", "seq", "guid"), P("req", "seq", "guid")),
        check_vma=False,
    )
```

```python
import functools

import jax
import jax.numpy as jnp
from jax import lax
from jax.experimental import pallas as pl
from jax.experimental.pallas import tpu as pltpu
from jax.sharding import PartitionSpec as P

HD = 64
STEPS = 28


norm_epsilon = 1e-06
flow_shift = 3.0
guide_scale = 4.5


def partner(value, axis, bit):
    mask = 2**bit
    pairs = [(source, source ^ mask) for source in range(lax.axis_size(axis))]
    return lax.ppermute(value, axis, pairs)


def modulate(values_in, shift_vec, scale_vec):
    values_in = values_in.astype(jnp.float32)
    average = jnp.mean(values_in, axis=-1, keepdims=True)
    variance = jnp.mean((values_in - average) ** 2, axis=-1, keepdims=True)
    normed = (values_in - average) * lax.rsqrt(variance + norm_epsilon)
    return (normed * (1.0 + scale_vec[..., None, :]) + shift_vec[..., None, :]).astype(jnp.bfloat16)


def sigma_level(step_value):
    remaining = 1.0 - step_value / STEPS
    return flow_shift * remaining / (1.0 + (flow_shift - 1.0) * remaining)


def local(
    img_hidden,
    txt_hidden,
    img_mod,
    txt_mod,
    w_img_qkv,
    w_txt_qkv,
    w_out,
    w_head,
    text_lengths,
    latent,
    step,
):
    prompts = img_hidden.shape[1]
    img_rows = img_hidden.shape[2]
    txt_rows = txt_hidden.shape[2]
    dev_rows = img_rows + txt_rows
    model_width = img_hidden.shape[3]
    image_in = modulate(img_hidden[0], img_mod[0, :, 0], img_mod[0, :, 1])
    text_in = modulate(txt_hidden[0], txt_mod[0, :, 0], txt_mod[0, :, 1])
    full_img, full_txt, full_head = (
        lax.all_gather(w_img_qkv, ("guid", "req", "seq"), axis=0, tiled=True),
        lax.all_gather(w_txt_qkv, ("guid", "req", "seq"), axis=0, tiled=True),
        lax.all_gather(w_head, ("guid", "req", "seq"), axis=0, tiled=True),
    )
    attn_width = full_img.shape[1] // 3
    head_count = attn_width // HD
    qkv_image = jnp.einsum(
        "prd,de->pre", image_in, full_img, preferred_element_type=jnp.float32
    ).astype(jnp.bfloat16)
    qkv_text = jnp.einsum(
        "prd,de->pre", text_in, full_txt, preferred_element_type=jnp.float32
    ).astype(jnp.bfloat16)
    query_rows = qkv_image[..., :attn_width]
    key_rows = jnp.concatenate(
        [qkv_image[..., attn_width : 2 * attn_width], qkv_text[..., attn_width : 2 * attn_width]],
        axis=1,
    )
    value_rows = jnp.concatenate(
        [qkv_image[..., 2 * attn_width :], qkv_text[..., 2 * attn_width :]], axis=1
    )
    lengths = text_lengths[0]
    query_heads = query_rows.reshape(prompts, img_rows, head_count, HD)
    running = jnp.full((prompts, head_count, img_rows), -1e30, jnp.float32)
    key_piece = lax.all_gather(key_rows, "seq", axis=1, tiled=True)
    value_piece = lax.all_gather(value_rows, "seq", axis=1, tiled=True)
    piece_rows = key_piece.shape[1]
    key_heads = key_piece.reshape(prompts, piece_rows, head_count, HD)
    value_heads = value_piece.reshape(prompts, piece_rows, head_count, HD)
    scores = (
        jnp.einsum("pqhd,pkhd->phqk", query_heads, key_heads, preferred_element_type=jnp.float32)
        * 0.125
    )
    position = jnp.arange(piece_rows, dtype=jnp.int32)
    owner_dev = position // dev_rows
    offset = position % dev_rows
    text_pos = owner_dev * txt_rows + offset - img_rows
    allowed = (offset < img_rows)[None, :] | (text_pos[None, :] < lengths[:, None])
    scores = jnp.where(allowed[:, None, None, :], scores, -1e30)
    newest = jnp.maximum(running, jnp.max(scores, axis=-1))
    weights = jnp.exp(scores - newest[..., None])
    totals = jnp.sum(weights, axis=-1)
    accumulated = jnp.einsum(
        "phqk,pkhd->phqd",
        weights.astype(jnp.bfloat16),
        value_heads,
        preferred_element_type=jnp.float32,
    )
    running, totals, accumulated = (newest, totals, accumulated)
    mixture = accumulated / totals[..., None]
    attended = (
        jnp.transpose(mixture, (0, 2, 1, 3))
        .reshape(prompts, img_rows, attn_width)
        .astype(jnp.bfloat16)
    )
    flattened = attended.reshape(prompts * img_rows, attn_width)
    full_out = lax.all_gather(w_out, ("guid", "req", "seq"), axis=0, tiled=True)
    projected = jnp.dot(flattened, full_out, preferred_element_type=jnp.float32)
    residual = img_hidden[0].astype(jnp.float32) + img_mod[0, :, 2][:, None, :] * projected.reshape(
        prompts, img_rows, model_width
    )
    final_in = modulate(residual, img_mod[0, :, 3], img_mod[0, :, 4])
    guid_index = lax.axis_index("guid")
    half_width = latent.shape[2]
    own_start = guid_index * half_width
    other_start = (1 - guid_index) * half_width
    whole_velocity = jnp.einsum(
        "prd,dc->prc", final_in, full_head, preferred_element_type=jnp.float32
    )
    own_velocity = lax.dynamic_slice_in_dim(whole_velocity, own_start, half_width, 2)
    partner_part = lax.dynamic_slice_in_dim(whole_velocity, other_start, half_width, 2)
    other_velocity = partner(partner_part.astype(jnp.bfloat16), "guid", 0).astype(
        partner_part.dtype
    )
    cond_velocity = jnp.where(guid_index == 0, own_velocity, other_velocity)
    free_velocity = jnp.where(guid_index == 0, other_velocity, own_velocity)
    guided = free_velocity + guide_scale * (cond_velocity - free_velocity)
    step_value = step[0].astype(jnp.float32)
    advanced = latent + (sigma_level(step_value + 1.0) - sigma_level(step_value)) * guided
    return (advanced, guided)


ALL_AXES = ("guid", "req", "seq")
LOG2E = 1.4426950408889634


def attend_kernel(images, texts, *refs):
    q_ref, o_ref = refs[0], refs[-1]
    pieces = []
    at = 1
    for _ in range(images):
        pieces.append((refs[at], refs[at + 1], None))
        at += 2
    for _ in range(texts):
        pieces.append((refs[at], refs[at + 1], refs[at + 2]))
        at += 3
    rows = q_ref.shape[0]
    sub = min(256, rows)
    lane = lax.broadcasted_iota(jnp.int32, (sub, 128), 1)
    units = [(start, head) for start in range(0, rows, sub) for head in range(2)]

    def score(start, head):
        q = q_ref[start : start + sub, :] * jnp.asarray(0.125, jnp.bfloat16)
        mine = (lane < HD) if head == 0 else (lane >= HD)
        q = jnp.where(mine, q, jnp.zeros_like(q))
        scores = []
        for k_ref, _, bias_ref in pieces:
            s = lax.dot_general(
                q, k_ref[...], (((1,), (1,)), ((), ())), preferred_element_type=jnp.float32
            )
            if bias_ref is not None:
                s = s + bias_ref[0:1, :]
            scores.append(s)
        return scores

    def mix(scores):
        top = functools.reduce(jnp.maximum, [jnp.max(s, axis=1, keepdims=True) for s in scores])
        top = top * LOG2E
        total = None
        mixed = None
        for s, (_, v_ref, _) in zip(scores, pieces):
            p = jnp.exp2(s * LOG2E - top)
            part = jnp.sum(p, axis=1, keepdims=True)
            total = part if total is None else total + part
            part = jnp.dot(p.astype(jnp.bfloat16), v_ref[...], preferred_element_type=jnp.float32)
            mixed = part if mixed is None else mixed + part
        return mixed / total

    halves = []
    ahead = score(*units[0])
    for index, (start, head) in enumerate(units):
        scores = ahead
        if index + 1 < len(units):
            ahead = score(*units[index + 1])
        halves.append(mix(scores))
        if head == 1:
            joined = jnp.where(lane < HD, halves[-2], halves[-1])
            o_ref[start : start + sub, :] = joined.astype(jnp.bfloat16)


def attend(query, width, images, texts):
    rows = query.shape[0]
    block = min(512, rows)
    pairs = width // 128
    args = [query]
    specs = [pl.BlockSpec((block, 128), lambda h, i: (i, h))]

    def column(array, start):
        args.append(array)
        specs.append(pl.BlockSpec((array.shape[0], 128), lambda h, i: (0, start // 128 + h)))

    keys = 0
    for array, key_at, value_at in images:
        column(array, key_at)
        column(array, value_at)
        keys += array.shape[0]
    for array, key_at, value_at, bias in texts:
        column(array, key_at)
        column(array, value_at)
        args.append(bias)
        specs.append(pl.BlockSpec(bias.shape, lambda h, i: (0, 0)))
        keys += array.shape[0]
    return pl.pallas_call(
        functools.partial(attend_kernel, len(images), len(texts)),
        grid=(pairs, rows // block),
        in_specs=specs,
        out_specs=pl.BlockSpec((block, 128), lambda h, i: (i, h)),
        out_shape=jax.ShapeDtypeStruct((rows, width), jnp.bfloat16),
        compiler_params=pltpu.CompilerParams(vmem_limit_bytes=32 * 2**20),
        cost_estimate=pl.CostEstimate(
            flops=16 * rows * keys * width,
            bytes_accessed=4 * (rows + keys) * width,
            transcendentals=rows * keys * width // HD,
        ),
    )(*args)


def text_bias(position, length):
    bias = jnp.where(position < length, 0.0, -1e30).astype(jnp.float32)
    return jnp.broadcast_to(bias[None, :], (8, bias.shape[0]))


def moved(
    img_hidden,
    txt_hidden,
    img_mod,
    txt_mod,
    w_img_qkv,
    w_txt_qkv,
    w_out,
    w_head,
    text_lengths,
    latent,
    step,
):
    ranks = lax.axis_size("seq")
    seq = lax.axis_index("seq")
    core = lax.axis_index("req") % 2
    guid = lax.axis_index("guid")
    attn_width = w_out.shape[0] * lax.axis_size(ALL_AXES)
    model_width = img_hidden.shape[3]
    img_rows, txt_rows = img_hidden.shape[2], txt_hidden.shape[2]
    img_half, txt_half = img_rows // 2, txt_rows // 2

    def swap(value):
        count = lax.axis_size("req")
        return lax.ppermute(value, "req", [(r, r ^ 1) for r in range(count)])

    def hop(value, k):
        return lax.ppermute(value, "seq", [(r, r ^ k) for r in range(ranks)])

    def pick(value, index):
        return lax.dynamic_index_in_dim(value, index, 0, keepdims=False)

    def spread(value):
        return [pick(value, seq)] + [hop(pick(value, seq ^ k), k) for k in range(1, ranks)]

    def by_core(mine, other, axis):
        return jnp.where(
            core == 0,
            jnp.concatenate([mine, other], axis),
            jnp.concatenate([other, mine], axis),
        )

    length_row = jnp.broadcast_to(
        text_lengths[0, ranks:].astype(jnp.float32)[:, None, None], (ranks // 2, 1, model_width)
    )
    facts = jnp.concatenate([img_mod[0, ranks:], txt_mod[0, ranks:], length_row], 1)
    facts = pick(by_core(facts, swap(facts), 0), seq)
    mods = img_mod.shape[2]
    mod_pair, tmod_pair = facts[:mods], facts[mods:-1]
    len_pair = facts[-1, 0].astype(jnp.int32)
    mod_own, tmod_own, len_own = pick(img_mod[0], seq), pick(txt_mod[0], seq), pick(text_lengths[0], seq)

    hidden = jnp.concatenate([img_hidden[0, :ranks], txt_hidden[0, :ranks]], 1)
    own_rows = spread(hidden)

    full_img = lax.all_gather(w_img_qkv, ALL_AXES, axis=0, tiled=True)
    txt_lines, full_img, own_rows = lax.optimization_barrier(
        (w_txt_qkv[:, attn_width:], full_img, own_rows)
    )
    full_txt = lax.all_gather(txt_lines, ALL_AXES, axis=0, tiled=True)

    kept = jnp.concatenate(
        [
            lax.dynamic_slice_in_dim(img_hidden[0, ranks:], core * img_half, img_half, 1),
            lax.dynamic_slice_in_dim(txt_hidden[0, ranks:], core * txt_half, txt_half, 1),
        ],
        1,
    )
    given = jnp.concatenate(
        [
            lax.dynamic_slice_in_dim(img_hidden[0, ranks:], (1 - core) * img_half, img_half, 1),
            lax.dynamic_slice_in_dim(txt_hidden[0, ranks:], (1 - core) * txt_half, txt_half, 1),
        ],
        1,
    )
    pair_rows = spread(by_core(kept, swap(given), 0))
    img_own = jnp.concatenate([r[:img_rows] for r in own_rows], 0)
    txt_own = jnp.concatenate([r[img_rows:] for r in own_rows], 0)
    img_pair = jnp.concatenate([r[:img_half] for r in pair_rows], 0)
    txt_pair = jnp.concatenate([r[img_half:] for r in pair_rows], 0)

    def dot(left, right):
        return jnp.dot(left, right, preferred_element_type=jnp.float32)

    def places(start, count):
        slots = jnp.arange(ranks, dtype=jnp.int32) ^ seq
        return (slots[:, None] * txt_rows + start + jnp.arange(count, dtype=jnp.int32)[None]).reshape(-1)

    qkv_own = dot(modulate(img_own, mod_own[0], mod_own[1]), full_img).astype(jnp.bfloat16)
    head_lines = w_head.size // model_width
    tail = jnp.concatenate([w_out, w_head.reshape(head_lines, model_width)], 0)
    tail, full_txt, qkv_own = lax.optimization_barrier((tail, full_txt, qkv_own))
    full_tail = lax.all_gather(tail, ALL_AXES, axis=0, tiled=False)
    full_out = full_tail[:, : w_out.shape[0]].reshape(attn_width, model_width)
    full_head = full_tail[:, w_out.shape[0] :].reshape(model_width, w_head.shape[1])
    kvt_own = dot(modulate(txt_own, tmod_own[0], tmod_own[1]), full_txt).astype(jnp.bfloat16)
    qkv_pair = dot(modulate(img_pair, mod_pair[0], mod_pair[1]), full_img).astype(jnp.bfloat16)
    kvt_pair = dot(modulate(txt_pair, tmod_pair[0], tmod_pair[1]), full_txt).astype(jnp.bfloat16)
    kv_other = swap(qkv_pair[:, attn_width:])
    kvt_other = swap(kvt_pair)

    attended_own = attend(
        qkv_own,
        attn_width,
        [(qkv_own, attn_width, 2 * attn_width)],
        [(kvt_own, 0, attn_width, text_bias(places(0, txt_rows), len_own))],
    )
    attended_pair = attend(
        qkv_pair,
        attn_width,
        [(qkv_pair, attn_width, 2 * attn_width), (kv_other, 0, attn_width)],
        [
            (kvt_pair, 0, attn_width, text_bias(places(core * txt_half, txt_half), len_pair)),
            (kvt_other, 0, attn_width, text_bias(places((1 - core) * txt_half, txt_half), len_pair)),
        ],
    )

    def finish(attended, hidden, mod):
        residual = hidden.astype(jnp.float32) + mod[2] * dot(attended, full_out)
        return dot(modulate(residual, mod[3], mod[4]), full_head)

    velocity = jnp.concatenate(
        [
            finish(attended_own, img_own, mod_own).reshape(ranks, img_rows, -1),
            finish(attended_pair, img_pair, mod_pair).reshape(ranks, img_half, -1),
        ],
        1,
    )
    part = latent.shape[2]
    own = lax.dynamic_slice_in_dim(velocity, guid * part, part, 2)
    sent = lax.dynamic_slice_in_dim(velocity, (1 - guid) * part, part, 2).astype(jnp.bfloat16)
    other = partner(sent, "guid", 0).astype(jnp.float32)
    cond = jnp.where(guid == 0, own, other)
    free = jnp.where(guid == 0, other, own)
    guided = free + guide_scale * (cond - free)
    back = jnp.stack([guided[0]] + [hop(guided[k], k) for k in range(1, ranks)])
    back = jnp.stack([pick(back, seq ^ p) for p in range(ranks)])
    shared = back[:, img_rows:]
    kept = lax.dynamic_slice_in_dim(shared, core * (ranks // 2), ranks // 2, 0)
    given = lax.dynamic_slice_in_dim(shared, (1 - core) * (ranks // 2), ranks // 2, 0)
    guided = jnp.concatenate([back[:, :img_rows], by_core(kept, swap(given), 1)], 0)
    step_value = step[0].astype(jnp.float32)
    advanced = latent + (sigma_level(step_value + 1.0) - sigma_level(step_value)) * guided
    return (advanced, guided)


def block(img_hidden, *others):
    ranks = lax.axis_size("seq")
    if ranks & (ranks - 1) == 0 and 2 * img_hidden.shape[1] == 3 * ranks and lax.axis_size("req") % 2 == 0:
        return moved(img_hidden, *others)
    return local(img_hidden, *others)


def solution(mesh):
    placed = (
        P("guid", "req", "seq", None),
        P("guid", "req", "seq", None),
        P("guid", "req", None, None),
        P("guid", "req", None, None),
        P(("guid", "req", "seq"), None),
        P(("guid", "req", "seq"), None),
        P(("guid", "req", "seq"), None),
        P(("guid", "req", "seq"), None),
        P("guid", "req"),
        P("req", "seq", "guid"),
        P(),
    )
    return jax.shard_map(
        block,
        mesh=mesh,
        in_specs=placed,
        out_specs=(P("req", "seq", "guid"), P("req", "seq", "guid")),
        check_vma=False,
    )
```
